32 devices in a mesh: groups: 2 (over y), dp: 16 (over z, x, core).
Axes of the slice: x: 2, y: 2, z: 4, core: 2. Of those that a mesh axis runs over, the one named last changes fastest.
Arguments:
- activations: bfloat16 [4096, 4096], P(('groups', 'dp')), parts along dimension 0
- gradients: bfloat16 [4096, 8, 1536], P(('groups', 'dp')), parts along dimension 0
- expert_ids: int32 [4096, 8], P(('groups', 'dp')), parts along dimension 0, may hold values from 0 to 127, all different within a row; in each aligned block of 128 rows (0 to 127, 128 to 255, ...) at most 16 rows name the same one
- window_experts: int32 [16], replicated, may hold values from 0 to 127, as said below
Outputs:
- input_factor: bfloat16 [131072, 4096], P(('groups', 'dp')), parts along dimension 0
- grad_factor: bfloat16 [49152, 1536], P(('groups', 'dp')), parts along dimension 0
The draws below stay inside these ranges and needn't reach their ends.
There are 2 independent parts, one for each index of `groups`. The reference program is written for one: setup_inputs(seed, part) draws one part's arguments, and reference() takes and returns one part's arrays. A program takes and returns all parts, laid end to end along the dimension named above; an argument that names none is the same for every part. Nothing has to cross between parts.
Inputs may be any that keep to these rules, and one draw needn't show every extreme that they name: `expert_ids`: each token names 8 different experts; in each aligned block of 128 tokens no expert is named by more than 16 tokens. `window_experts`: 16 different experts.
All inputs are finite; a program needn't handle non-finite values.
Results may differ from the reference program's by a relative error of at most 0.001.
Values may be sent and summed in bfloat16 or wider, within the bound.
A program may use at most 256 MiB of HBM per device.

```python
import math
import jax
import jax.numpy as jnp
import numpy as np
from jax import lax

D = 4096
FF = 1536
EXPERTS = 128
TOPK = 8
WIN = 16
TOKENS = 2048
BLOCK = 128
SLOT = 16
N_DP = 16


def feature_scaled(key, rows, width):
    base_key, column_key = jax.random.split(key, 2)
    base = jax.random.normal(base_key, (rows, width), jnp.float32)
    trend = 0.7 + 0.6 * jnp.arange(width, dtype=jnp.float32) / width
    jitter = jnp.exp(jax.random.uniform(column_key, (width,), jnp.float32, math.log(0.7), math.log(1.4)))
    return base * (trend * jitter)[None, :]


def draw_activations(key, part):
    key = jax.random.fold_in(key, 11)
    return feature_scaled(key, TOKENS, D).astype(jnp.bfloat16)


def draw_gradients(key, part):
    key = jax.random.fold_in(key, 23)
    return feature_scaled(key, TOKENS * TOPK, FF).reshape(TOKENS, TOPK, FF).astype(jnp.bfloat16)


def draw_window_experts(key, part):
    key = jax.random.fold_in(key, 37)
    return jax.random.permutation(key, EXPERTS)[:WIN].astype(jnp.int32)


def shared_out(stream_key, own, number, rows, count, top, limit, slope):
    order = jax.random.permutation(stream_key, count)
    packed, ordinary = portions_of(count, rows * top, limit, slope, True), portions_of(count, rows * top, limit, slope, False)
    places = jnp.arange(count)

    def named(sizes, offset_by):
        used = int((sizes > 0).sum())
        fixed = max(1, used // 4)
        moved = fixed + (places - fixed + offset_by * (used - fixed)) % max(1, count - fixed)
        return jnp.zeros((count,), jnp.int32).at[order[jnp.where(places < fixed, places, moved)]].set(jnp.asarray(sizes, jnp.int32))

    sizes = jnp.where(number % 4 == 0, named(packed, number // 4), named(ordinary, number - number // 4 - 1))
    mixed = jax.random.permutation(jax.random.fold_in(own, 3), count)
    source_of, taker = mixed[0:count // 2 * 2:2], mixed[1:count // 2 * 2:2]
    margin = jnp.minimum(sizes[source_of] - 1, limit - sizes[taker]) // 2
    margin = jnp.where((source_of == order[0]) | (taker == order[0]) | (sizes[taker] == 0), 0, jnp.maximum(margin, 0))
    moved = jax.random.randint(jax.random.fold_in(own, 4), (count // 2,), 0, 1 << 20) % (margin + 1)
    sizes = sizes.at[source_of].add(-moved).at[taker].add(moved)
    members = jnp.searchsorted(jnp.cumsum(sizes), jnp.arange(rows * top), side="right").astype(jnp.int32)
    listing = members.reshape(top, rows).T
    listing = listing[jax.random.permutation(jax.random.fold_in(own, 1), rows)]
    offset_by = jax.random.randint(jax.random.fold_in(own, 2), (rows, 1), 0, top)
    return jnp.take_along_axis(listing, (jnp.arange(top)[None, :] + offset_by) % top, axis=1)


def portions_of(count, total, bound, lean, full):
    weights = [(1 << 20) // math.isqrt(standing ** lean) + 1 for standing in range(1, count + 1)]
    largest = bound if full else min(bound, max(-(-total // count), total * weights[0] // sum(weights)))
    least = 1 if total - largest >= count - 1 else 0
    holding, rest = [largest] + [least] * (count - 1), total - largest - least * (count - 1)
    while rest > 0:
        candidates = [i for i in range(1, count) if holding[i] < largest] or [i for i in range(1, count) if holding[i] < bound]
        whole, budget = sum([weights[i] for i in candidates]), rest
        for i in candidates:
            addition = min(bound - holding[i], max(1, budget * weights[i] // whole), rest)
            holding[i] = holding[i] + addition
            rest = rest - addition
    return np.array(holding)


def setup_inputs(seed: int = 0, part: int = 0) -> dict:
    seeds = jax.random.split(jax.random.key(seed), 5)
    part_splits = jax.random.split(jax.random.fold_in(seeds[4], part), 5)
    activations = draw_activations(jax.random.fold_in(jax.random.fold_in(seeds[4], part), 71), part)
    gradients = draw_gradients(jax.random.fold_in(jax.random.fold_in(seeds[4], part), 71), part)
    expert_ids_keys = jax.random.split(jax.random.fold_in(part_splits[2], 1), TOKENS // BLOCK)
    expert_ids_turns = jax.random.permutation(jax.random.fold_in(part_splits[2], 3), TOKENS // BLOCK)
    expert_ids = jax.vmap(lambda own, number: shared_out(jax.random.fold_in(part_splits[2], 2), own, number, BLOCK, EXPERTS, TOPK, SLOT, 2))(expert_ids_keys, expert_ids_turns).reshape((TOKENS, TOPK))
    window_experts = draw_window_experts(jax.random.fold_in(seeds[4], 71), part)
    return {"activations": activations, "gradients": gradients, "expert_ids": expert_ids, "window_experts": window_experts}


damping_share = 1.0


def damped_factor(gram, row_count, width):
    scaled = gram / row_count
    shift = damping_share * jnp.trace(scaled) / width
    return (scaled + shift * jnp.eye(width, dtype=jnp.float32)).astype(jnp.bfloat16)


def reference(activations, gradients, expert_ids, window_experts):
    flat_ids = expert_ids.reshape(-1)
    capacity = N_DP * (N_DP // WIN) * SLOT
    act_padded = jnp.concatenate([activations, jnp.zeros((1, D), jnp.bfloat16)], axis=0)
    grad_padded = jnp.concatenate([gradients.reshape(TOKENS * TOPK, FF), jnp.zeros((1, FF), jnp.bfloat16)], axis=0)

    def one_expert(expert):
        selected = flat_ids == expert
        positions = jnp.nonzero(selected, size=capacity, fill_value=TOKENS * TOPK)[0].astype(jnp.int32)
        row_count = jnp.sum(selected.astype(jnp.float32))
        act_rows = act_padded[positions // TOPK]
        grad_rows = grad_padded[positions]
        gram_in = jnp.dot(act_rows.T, act_rows, preferred_element_type=jnp.float32)
        gram_grad = jnp.dot(grad_rows.T, grad_rows, preferred_element_type=jnp.float32)
        return damped_factor(gram_in, row_count, D), damped_factor(gram_grad, row_count, FF)

    input_stack, grad_stack = lax.map(one_expert, window_experts)
    return input_stack.reshape(WIN * D, D), grad_stack.reshape(WIN * FF, FF)
```

```python
import functools

import jax
import jax.numpy as jnp
from jax import lax
from jax.experimental import pallas as pl
from jax.experimental.pallas import tpu as pltpu
from jax.sharding import PartitionSpec as P

EXPERTS = 128
TOPK = 8
WIN = 16
FLAG = 128


damping_share = 1.0


def row_tile(span):
    for tile in (512, 256, 128):
        if span % tile == 0:
            return tile
    return span


def factor_kernel(width, tile, chunk, aligned, start_ref, total_ref, left_ref, rows_ref, out_ref, shift_ref):
    step = pl.program_id(0)
    depth = rows_ref.shape[0]
    inverse = 1.0 / total_ref[0]

    @pl.when(step == 0)
    def _():
        def add(i, sums):
            part = rows_ref[pl.ds(pl.multiple_of(i * 16, 16), 16), :width].astype(jnp.float32)
            return sums + part * part

        sums = lax.fori_loop(0, depth // 16, add, jnp.zeros((16, width), jnp.float32))
        shift_ref[0] = damping_share * jnp.sum(sums) * inverse / width

    left = left_ref[...]
    dims = (((0,), (0,)), ((), ()))

    def scaled(columns):
        part = lax.dot_general(left, rows_ref[:, columns], dims, preferred_element_type=jnp.float32)
        return part * inverse

    def damped(value, first_row, first_column):
        down = lax.broadcasted_iota(jnp.int32, value.shape, 0) + first_row
        across = lax.broadcasted_iota(jnp.int32, value.shape, 1) + first_column
        return value + jnp.where(down == across, shift_ref[0], 0.0)

    first_row = start_ref[0] + step * tile
    for column in range(0, width, chunk):
        columns = pl.ds(column, chunk)
        value = scaled(columns)
        if not aligned:
            value = damped(value, first_row, column)
        out_ref[:, columns] = value.astype(jnp.bfloat16)
    if aligned:
        columns = pl.ds(pl.multiple_of(step * tile, tile), tile)
        out_ref[:, columns] = damped(scaled(columns), 0, 0).astype(jnp.bfloat16)


def factor(rows, width, total, block_index, group_size, name):
    depth = rows.shape[0]
    span = width // group_size
    tile = row_tile(span)
    aligned = group_size == 1
    left = rows if aligned else lax.dynamic_slice_in_dim(rows, block_index * span, span, 1)
    return pl.pallas_call(
        functools.partial(factor_kernel, width, tile, 512, aligned),
        out_shape=jax.ShapeDtypeStruct((span, width), jnp.bfloat16),
        grid=(span // tile,),
        in_specs=[
            pl.BlockSpec(memory_space=pltpu.SMEM),
            pl.BlockSpec(memory_space=pltpu.SMEM),
            pl.BlockSpec((depth, tile), lambda i: (0, i)),
            pl.BlockSpec(rows.shape, lambda i: (0, 0)),
        ],
        out_specs=pl.BlockSpec((tile, width), lambda i: (i, 0)),
        scratch_shapes=[pltpu.SMEM((1,), jnp.float32)],
        compiler_params=pltpu.CompilerParams(vmem_limit_bytes=56 * 1024 * 1024),
        cost_estimate=pl.CostEstimate(
            flops=2 * depth * span * width, bytes_accessed=2 * span * width + 2 * depth * width, transcendentals=0
        ),
        name=name,
    )((block_index * span).astype(jnp.int32).reshape(1), total.reshape(1), left, rows)


def shards(activations, gradients, expert_ids, window_experts):
    devices = lax.axis_size("dp")
    group_size = devices // WIN
    tok_rows = activations.shape[0]
    block_rows = tok_rows // group_size
    slot_rows = max(2, 2 * block_rows * TOPK // EXPERTS)
    width_in = activations.shape[1]
    width_grad = gradients.shape[2]
    pair_rows = block_rows * TOPK
    matched = (expert_ids[:, :, None] == window_experts[None, None, :]).astype(jnp.int32)
    matched = matched.reshape(group_size, pair_rows, WIN)
    upper = (jnp.arange(pair_rows)[:, None] <= jnp.arange(pair_rows)[None, :]).astype(jnp.bfloat16)
    running = jnp.einsum(
        "gaw,ab->gbw", matched.astype(jnp.bfloat16), upper, preferred_element_type=jnp.float32
    )
    ordinal = running - 1.0
    placed = (matched[..., None] == 1) & (
        ordinal[..., None] == jnp.arange(slot_rows, dtype=jnp.float32)[None, None, None, :]
    )
    chosen = placed.astype(jnp.bfloat16)
    token_chosen = jnp.sum(chosen.reshape(group_size, block_rows, TOPK, WIN, slot_rows), axis=2)
    in_sorted = jnp.einsum(
        "gtws,gtd->wgsd",
        token_chosen,
        activations.reshape(group_size, block_rows, width_in),
        preferred_element_type=jnp.float32,
    ).astype(jnp.bfloat16)
    grad_sorted = jnp.einsum(
        "gaws,gaf->wgsf",
        chosen,
        gradients.reshape(group_size, pair_rows, width_grad),
        preferred_element_type=jnp.float32,
    ).astype(jnp.bfloat16)
    flags = jnp.sum(token_chosen, axis=1).transpose(1, 0, 2)[..., None]
    in_sorted = jnp.concatenate(
        [in_sorted, jnp.broadcast_to(flags, in_sorted.shape[:3] + (FLAG,))], axis=3
    )
    copies_in = jnp.repeat(
        in_sorted.reshape(WIN, group_size * slot_rows, width_in + FLAG), group_size, axis=0
    )
    copies_grad = jnp.repeat(
        grad_sorted.reshape(WIN, group_size * slot_rows, width_grad), group_size, axis=0
    )
    in_rows = lax.all_to_all(copies_in, "dp", split_axis=0, concat_axis=0, tiled=True)
    grad_rows = lax.all_to_all(copies_grad, "dp", split_axis=0, concat_axis=0, tiled=True)
    in_rows = in_rows.reshape(-1, width_in + FLAG)
    grad_rows = grad_rows.reshape(-1, width_grad)
    total = jnp.sum(in_rows[:, width_in].astype(jnp.float32))
    block_index = lax.axis_index("dp") % group_size
    return (
        factor(in_rows, width_in, total, block_index, group_size, "input_factor"),
        factor(grad_rows, width_grad, total, block_index, group_size, "grad_factor"),
    )


def solution(mesh):
    placed = (
        P(("groups", "dp"), None),
        P(("groups", "dp"), None, None),
        P(("groups", "dp"), None),
        P(),
    )
    return jax.shard_map(
        shards,
        mesh=mesh,
        in_specs=placed,
        out_specs=(P(("groups", "dp"), None), P(("groups", "dp"), None)),
        check_vma=False,
    )
```

```python
import functools

import jax
import jax.numpy as jnp
from jax import lax
from jax.experimental import pallas as pl
from jax.experimental.pallas import tpu as pltpu
from jax.sharding import PartitionSpec as P

EXPERTS = 128
TOPK = 8
WIN = 16
FLAG = 128


damping_share = 1.0


def row_tile(span):
    for tile in (512, 256, 128):
        if span % tile == 0:
            return tile
    return span


def factor_kernel(width, tile, chunk, aligned, start_ref, flags_ref, left_ref, rows_ref, out_ref, scale_ref):
    step = pl.program_id(0)
    depth = rows_ref.shape[0]
    piece = min(depth, 128)

    @pl.when(step == 0)
    def _():
        def add(i, sums):
            rows = pl.ds(pl.multiple_of(i * piece, piece), piece)
            out = []
            for column, before in zip(range(0, width, chunk), sums):
                part = rows_ref[rows, column:column + chunk].astype(jnp.float32)
                out.append(before + jnp.sum((part * part).reshape(piece // 8, 8, chunk), axis=0))
            return out

        zeros = [jnp.zeros((8, chunk), jnp.float32)] * (width // chunk)
        sums = lax.fori_loop(0, depth // piece, add, zeros)
        whole = functools.reduce(lambda x, y: x + y, sums)
        inverse = FLAG / jnp.sum(flags_ref[...].astype(jnp.float32))
        scale_ref[0] = inverse
        scale_ref[1] = damping_share * jnp.sum(whole) * inverse / width

    inverse = scale_ref[0]
    left = left_ref[...].T

    def scaled(block, columns):
        return jnp.dot(block, rows_ref[:, columns], preferred_element_type=jnp.float32) * inverse

    def damped(value, first_row, first_column):
        down = lax.broadcasted_iota(jnp.int32, value.shape, 0) + first_row
        across = lax.broadcasted_iota(jnp.int32, value.shape, 1) + first_column
        return value + jnp.where(down == across, scale_ref[1], 0.0)

    first_row = start_ref[0] + step * tile
    for column in range(0, width, chunk):
        columns = pl.ds(column, chunk)
        value = scaled(left, columns)
        if not aligned:
            value = damped(value, first_row, column)
        out_ref[:, columns] = value.astype(jnp.bfloat16)
    if aligned:
        side = min(tile, 256)
        for down in range(0, tile, side):
            columns = pl.ds(pl.multiple_of(step * tile + down, side), side)
            value = damped(scaled(left[down:down + side], columns), 0, 0)
            out_ref[pl.ds(down, side), columns] = value.astype(jnp.bfloat16)


def select_kernel(block_rows, slot_rows, ids_ref, window_ref, act_ref, out_ref):
    tokens, width = act_ref.shape
    per_expert = tokens // block_rows * slot_rows
    rows = WIN * per_expert

    def iota(shape, dim):
        return lax.broadcasted_iota(jnp.int32, shape, dim)

    ids, window = ids_ref[...], window_ref[...]
    matched = jnp.zeros((tokens, WIN), jnp.float32)
    for k in range(ids.shape[1]):
        matched += jnp.where(ids[:, k:k + 1] == window, 1.0, 0.0)
    matched = matched.astype(jnp.bfloat16)
    later, earlier = iota((tokens, tokens), 0), iota((tokens, tokens), 1)
    before = (earlier < later) & (earlier // block_rows == later // block_rows)
    place = jnp.dot(
        jnp.where(before, 1.0, 0.0).astype(jnp.bfloat16), matched, preferred_element_type=jnp.float32
    ).astype(jnp.bfloat16)
    spread = jnp.where(iota((rows, WIN), 0) // per_expert == iota((rows, WIN), 1), 1.0, 0.0).astype(jnp.bfloat16)
    dims = (((1,), (1,)), ((), ()))
    hit = lax.dot_general(spread, matched, dims, preferred_element_type=jnp.float32)
    position = lax.dot_general(spread, place, dims, preferred_element_type=jnp.float32)
    row, token = iota((rows, tokens), 0), iota((rows, tokens), 1)
    inside = row % per_expert
    taken = (
        (hit > 0.5)
        & (position.astype(jnp.int32) == inside % slot_rows)
        & (token // block_rows == inside // slot_rows)
    )
    chosen = jnp.where(taken, 1.0, 0.0)
    flags = jnp.sum(chosen, axis=1, keepdims=True)
    out_ref[:, width:] = jnp.broadcast_to(flags, (rows, FLAG)).astype(jnp.bfloat16)
    chosen = chosen.astype(jnp.bfloat16)
    for column in range(0, width, 512):
        columns = pl.ds(column, 512)
        out_ref[:, columns] = jnp.dot(
            chosen, act_ref[:, columns], preferred_element_type=jnp.float32
        ).astype(jnp.bfloat16)


def select_rows(expert_ids, window_experts, activations, block_rows, slot_rows):
    tokens, width = activations.shape
    per_expert = tokens // block_rows * slot_rows
    return pl.pallas_call(
        functools.partial(select_kernel, block_rows, slot_rows),
        out_shape=jax.ShapeDtypeStruct((WIN * per_expert, width + FLAG), jnp.bfloat16),
        in_specs=[pl.BlockSpec(memory_space=pltpu.VMEM)] * 3,
        out_specs=pl.BlockSpec(memory_space=pltpu.VMEM),
        compiler_params=pltpu.CompilerParams(vmem_limit_bytes=32 * 1024 * 1024),
        cost_estimate=pl.CostEstimate(
            flops=2 * WIN * per_expert * tokens * width, bytes_accessed=6 * tokens * width, transcendentals=0
        ),
        name="select_rows",
    )(expert_ids, window_experts.reshape(1, WIN), activations)


def factor(rows, width, flagged, block_index, group_size, name):
    depth = rows.shape[0]
    span = width // group_size
    tile = row_tile(span)
    aligned = group_size == 1
    left = rows if aligned else lax.dynamic_slice_in_dim(rows, block_index * span, span, 1)
    return pl.pallas_call(
        functools.partial(factor_kernel, width, tile, 512, aligned),
        out_shape=jax.ShapeDtypeStruct((span, width), jnp.bfloat16),
        grid=(span // tile,),
        in_specs=[
            pl.BlockSpec(memory_space=pltpu.SMEM),
            pl.BlockSpec((depth, FLAG), lambda i: (0, flagged.shape[1] // FLAG - 1)),
            pl.BlockSpec((depth, tile), lambda i: (0, i)),
            pl.BlockSpec(rows.shape, lambda i: (0, 0)),
        ],
        out_specs=pl.BlockSpec((tile, width), lambda i: (i, 0)),
        scratch_shapes=[pltpu.SMEM((2,), jnp.float32)],
        compiler_params=pltpu.CompilerParams(vmem_limit_bytes=56 * 1024 * 1024),
        cost_estimate=pl.CostEstimate(
            flops=2 * depth * span * width, bytes_accessed=2 * span * width + 2 * depth * width, transcendentals=0
        ),
        name=name,
    )((block_index * span).astype(jnp.int32).reshape(1), flagged, left, rows)


def shards(activations, gradients, expert_ids, window_experts):
    devices = lax.axis_size("dp")
    group_size = devices // WIN
    tok_rows = activations.shape[0]
    block_rows = tok_rows // group_size
    slot_rows = max(2, 2 * block_rows * TOPK // EXPERTS)
    width_in = activations.shape[1]
    width_grad = gradients.shape[2]
    pair_rows = block_rows * TOPK
    matched = (expert_ids[:, :, None] == window_experts[None, None, :]).astype(jnp.int32)
    matched = matched.reshape(group_size, pair_rows, WIN)
    upper = (jnp.arange(pair_rows)[:, None] <= jnp.arange(pair_rows)[None, :]).astype(jnp.bfloat16)
    running = jnp.einsum(
        "gaw,ab->gbw", matched.astype(jnp.bfloat16), upper, preferred_element_type=jnp.float32
    )
    ordinal = running - 1.0
    placed = (matched[..., None] == 1) & (
        ordinal[..., None] == jnp.arange(slot_rows, dtype=jnp.float32)[None, None, None, :]
    )
    chosen = placed.astype(jnp.bfloat16)
    in_sorted = select_rows(expert_ids, window_experts, activations, block_rows, slot_rows)
    grad_sorted = jnp.einsum(
        "gaws,gaf->wgsf",
        chosen,
        gradients.reshape(group_size, pair_rows, width_grad),
        preferred_element_type=jnp.float32,
    ).astype(jnp.bfloat16)
    copies_in = jnp.repeat(
        in_sorted.reshape(WIN, group_size * slot_rows, width_in + FLAG), group_size, axis=0
    )
    copies_grad = jnp.repeat(
        grad_sorted.reshape(WIN, group_size * slot_rows, width_grad), group_size, axis=0
    )
    in_rows = lax.all_to_all(copies_in, "dp", split_axis=0, concat_axis=0, tiled=True)
    grad_rows = lax.all_to_all(copies_grad, "dp", split_axis=0, concat_axis=0, tiled=True)
    in_rows = in_rows.reshape(-1, width_in + FLAG)
    grad_rows = grad_rows.reshape(-1, width_grad)
    block_index = lax.axis_index("dp") % group_size
    return (
        factor(in_rows, width_in, in_rows, block_index, group_size, "input_factor"),
        factor(grad_rows, width_grad, in_rows, block_index, group_size, "grad_factor"),
    )


def solution(mesh):
    placed = (
        P(("groups", "dp"), None),
        P(("groups", "dp"), None, None),
        P(("groups", "dp"), None),
        P(),
    )
    return jax.shard_map(
        shards,
        mesh=mesh,
        in_specs=placed,
        out_specs=(P(("groups", "dp"), None), P(("groups", "dp"), None)),
        check_vma=False,
    )
```

```python
import functools

import jax
import jax.numpy as jnp
from jax import lax
from jax.experimental import pallas as pl
from jax.experimental.pallas import tpu as pltpu
from jax.sharding import PartitionSpec as P

EXPERTS = 128
TOPK = 8
WIN = 16
FLAG = 128


damping_share = 1.0


def row_tile(span, width):
    for tile in (512, 256):
        if span % tile == 0 and tile * 4 <= max(width, 1024):
            return tile
    return span


def factor_kernel(width, tile, chunk, aligned, start_ref, flags_ref, left_ref, rows_ref, out_ref, scale_ref):
    step = pl.program_id(0)
    depth = rows_ref.shape[0]
    piece = min(depth, 128)

    @pl.when(step == 0)
    def _():
        def add(i, sums):
            rows = pl.ds(pl.multiple_of(i * piece, piece), piece)
            out = []
            for column, before in zip(range(0, width, chunk), sums):
                part = rows_ref[rows, column:column + chunk].astype(jnp.float32)
                out.append(before + jnp.sum((part * part).reshape(piece // 8, 8, chunk), axis=0))
            return out

        zeros = [jnp.zeros((8, chunk), jnp.float32)] * (width // chunk)
        sums = lax.fori_loop(0, depth // piece, add, zeros)
        whole = functools.reduce(lambda x, y: x + y, sums)
        inverse = FLAG / jnp.sum(flags_ref[...].astype(jnp.float32))
        scale_ref[0] = inverse
        scale_ref[1] = damping_share * jnp.sum(whole) * inverse / width

    inverse = scale_ref[0]
    left = left_ref[...].T

    def scaled(block, columns):
        return jnp.dot(block, rows_ref[:, columns], preferred_element_type=jnp.float32) * inverse

    def damped(value, first_row, first_column):
        down = lax.broadcasted_iota(jnp.int32, value.shape, 0) + first_row
        across = lax.broadcasted_iota(jnp.int32, value.shape, 1) + first_column
        return value + jnp.where(down == across, scale_ref[1], 0.0)

    first_row = start_ref[0] + step * tile
    for column in range(0, width, chunk):
        columns = pl.ds(column, chunk)
        value = scaled(left, columns)
        if not aligned:
            value = damped(value, first_row, column)
        out_ref[:, columns] = value.astype(jnp.bfloat16)
    if aligned:
        side = min(tile, 256)
        for down in range(0, tile, side):
            columns = pl.ds(pl.multiple_of(step * tile + down, side), side)
            value = damped(scaled(left[down:down + side], columns), 0, 0)
            out_ref[pl.ds(down, side), columns] = value.astype(jnp.bfloat16)


def select_kernel(block_rows, slot_rows, ids_ref, window_ref, act_ref, out_ref):
    tokens, width = act_ref.shape
    per_expert = tokens // block_rows * slot_rows
    rows = WIN * per_expert

    def iota(shape, dim):
        return lax.broadcasted_iota(jnp.int32, shape, dim)

    ids, window = ids_ref[...], window_ref[...]
    matched = jnp.zeros((tokens, WIN), jnp.float32)
    for k in range(ids.shape[1]):
        matched += jnp.where(ids[:, k:k + 1] == window, 1.0, 0.0)
    matched = matched.astype(jnp.bfloat16)
    later, earlier = iota((tokens, tokens), 0), iota((tokens, tokens), 1)
    before = (earlier < later) & (earlier // block_rows == later // block_rows)
    place = jnp.dot(
        jnp.where(before, 1.0, 0.0).astype(jnp.bfloat16), matched, preferred_element_type=jnp.float32
    ).astype(jnp.bfloat16)
    spread = jnp.where(iota((rows, WIN), 0) // per_expert == iota((rows, WIN), 1), 1.0, 0.0).astype(jnp.bfloat16)
    dims = (((1,), (1,)), ((), ()))
    hit = lax.dot_general(spread, matched, dims, preferred_element_type=jnp.float32)
    position = lax.dot_general(spread, place, dims, preferred_element_type=jnp.float32)
    row, token = iota((rows, tokens), 0), iota((rows, tokens), 1)
    inside = row % per_expert
    taken = (
        (hit > 0.5)
        & (position.astype(jnp.int32) == inside % slot_rows)
        & (token // block_rows == inside // slot_rows)
    )
    chosen = jnp.where(taken, 1.0, 0.0)
    flags = jnp.sum(chosen, axis=1, keepdims=True)
    out_ref[:, width:] = jnp.broadcast_to(flags, (rows, FLAG)).astype(jnp.bfloat16)
    chosen = chosen.astype(jnp.bfloat16)
    for column in range(0, width, 512):
        columns = pl.ds(column, 512)
        out_ref[:, columns] = jnp.dot(
            chosen, act_ref[:, columns], preferred_element_type=jnp.float32
        ).astype(jnp.bfloat16)


def select_rows(expert_ids, window_experts, activations, block_rows, slot_rows):
    tokens, width = activations.shape
    per_expert = tokens // block_rows * slot_rows
    return pl.pallas_call(
        functools.partial(select_kernel, block_rows, slot_rows),
        out_shape=jax.ShapeDtypeStruct((WIN * per_expert, width + FLAG), jnp.bfloat16),
        in_specs=[pl.BlockSpec(memory_space=pltpu.VMEM)] * 3,
        out_specs=pl.BlockSpec(memory_space=pltpu.VMEM),
        compiler_params=pltpu.CompilerParams(vmem_limit_bytes=32 * 1024 * 1024),
        cost_estimate=pl.CostEstimate(
            flops=2 * WIN * per_expert * tokens * width, bytes_accessed=6 * tokens * width, transcendentals=0
        ),
        name="select_rows",
    )(expert_ids, window_experts.reshape(1, WIN), activations)


def factor(rows, width, flagged, block_index, group_size, name):
    depth = rows.shape[0]
    span = width // group_size
    tile = row_tile(span, width)
    aligned = group_size == 1
    left = rows if aligned else lax.dynamic_slice_in_dim(rows, block_index * span, span, 1)
    return pl.pallas_call(
        functools.partial(factor_kernel, width, tile, 512, aligned),
        out_shape=jax.ShapeDtypeStruct((span, width), jnp.bfloat16),
        grid=(span // tile,),
        in_specs=[
            pl.BlockSpec(memory_space=pltpu.SMEM),
            pl.BlockSpec((depth, FLAG), lambda i: (0, flagged.shape[1] // FLAG - 1)),
            pl.BlockSpec((depth, tile), lambda i: (0, i)),
            pl.BlockSpec(rows.shape, lambda i: (0, 0)),
        ],
        out_specs=pl.BlockSpec((tile, width), lambda i: (i, 0)),
        scratch_shapes=[pltpu.SMEM((2,), jnp.float32)],
        compiler_params=pltpu.CompilerParams(vmem_limit_bytes=56 * 1024 * 1024),
        cost_estimate=pl.CostEstimate(
            flops=2 * depth * span * width, bytes_accessed=2 * span * width + 2 * depth * width, transcendentals=0
        ),
        name=name,
    )((block_index * span).astype(jnp.int32).reshape(1), flagged, left, rows)


def shards(activations, gradients, expert_ids, window_experts):
    devices = lax.axis_size("dp")
    group_size = devices // WIN
    tok_rows = activations.shape[0]
    block_rows = tok_rows // group_size
    slot_rows = max(2, 2 * block_rows * TOPK // EXPERTS)
    width_in = activations.shape[1]
    width_grad = gradients.shape[2]
    pair_rows = block_rows * TOPK
    matched = (expert_ids[:, :, None] == window_experts[None, None, :]).astype(jnp.int32)
    matched = matched.reshape(group_size, pair_rows, WIN)
    upper = (jnp.arange(pair_rows)[:, None] <= jnp.arange(pair_rows)[None, :]).astype(jnp.bfloat16)
    running = jnp.einsum(
        "gaw,ab->gbw", matched.astype(jnp.bfloat16), upper, preferred_element_type=jnp.float32
    )
    ordinal = running - 1.0
    placed = (matched[..., None] == 1) & (
        ordinal[..., None] == jnp.arange(slot_rows, dtype=jnp.float32)[None, None, None, :]
    )
    chosen = placed.astype(jnp.bfloat16)
    in_sorted = select_rows(expert_ids, window_experts, activations, block_rows, slot_rows)
    grad_sorted = jnp.einsum(
        "gaws,gaf->wgsf",
        chosen,
        gradients.reshape(group_size, pair_rows, width_grad),
        preferred_element_type=jnp.float32,
    ).astype(jnp.bfloat16)
    copies_in = jnp.repeat(
        in_sorted.reshape(WIN, group_size * slot_rows, width_in + FLAG), group_size, axis=0
    )
    copies_grad = jnp.repeat(
        grad_sorted.reshape(WIN, group_size * slot_rows, width_grad), group_size, axis=0
    )
    in_rows = lax.all_to_all(copies_in, "dp", split_axis=0, concat_axis=0, tiled=True)
    grad_rows = lax.all_to_all(copies_grad, "dp", split_axis=0, concat_axis=0, tiled=True)
    in_rows = in_rows.reshape(-1, width_in + FLAG)
    grad_rows = grad_rows.reshape(-1, width_grad)
    block_index = lax.axis_index("dp") % group_size
    return (
        factor(in_rows, width_in, in_rows, block_index, group_size, "input_factor"),
        factor(grad_rows, width_grad, in_rows, block_index, group_size, "grad_factor"),
    )


def solution(mesh):
    placed = (
        P(("groups", "dp"), None),
        P(("groups", "dp"), None, None),
        P(("groups", "dp"), None),
        P(),
    )
    return jax.shard_map(
        shards,
        mesh=mesh,
        in_specs=placed,
        out_specs=(P(("groups", "dp"), None), P(("groups", "dp"), None)),
        check_vma=False,
    )
```

```python
import functools

import jax
import jax.numpy as jnp
from jax import lax
from jax.experimental import pallas as pl
from jax.experimental.pallas import tpu as pltpu
from jax.sharding import PartitionSpec as P

EXPERTS = 128
TOPK = 8
WIN = 16
FLAG = 128


damping_share = 1.0


def row_tile(span):
    for tile in (512, 256, 128):
        if span % tile == 0:
            return tile
    return span


def factor_kernel(width, tile, chunk, aligned, first, start_ref, flags_ref, left_ref, rows_ref, *rest):
    out_ref, scale_ref = rest[-2:]
    step = pl.program_id(0) + first
    depth = rows_ref.shape[0]
    piece = min(depth, 128)

    @pl.when(step == first)
    def _():
        def add(i, sums):
            rows = pl.ds(pl.multiple_of(i * piece, piece), piece)
            out = []
            for column, before in zip(range(0, width, chunk), sums):
                part = rows_ref[rows, column:column + chunk].astype(jnp.float32)
                out.append(before + jnp.sum((part * part).reshape(piece // 8, 8, chunk), axis=0))
            return out

        zeros = [jnp.zeros((8, chunk), jnp.float32)] * (width // chunk)
        sums = lax.fori_loop(0, depth // piece, add, zeros)
        whole = functools.reduce(lambda x, y: x + y, sums)
        inverse = FLAG / jnp.sum(flags_ref[...].astype(jnp.float32))
        scale_ref[0] = inverse
        scale_ref[1] = damping_share * jnp.sum(whole) * inverse / width

    inverse = scale_ref[0]
    left = left_ref[...].T

    def scaled(block, columns):
        return jnp.dot(block, rows_ref[:, columns], preferred_element_type=jnp.float32) * inverse

    def damped(value, first_row, first_column):
        down = lax.broadcasted_iota(jnp.int32, value.shape, 0) + first_row
        across = lax.broadcasted_iota(jnp.int32, value.shape, 1) + first_column
        return value + jnp.where(down == across, scale_ref[1], 0.0)

    first_row = start_ref[0] + step * tile
    for column in range(0, width, chunk):
        columns = pl.ds(column, chunk)
        value = scaled(left, columns)
        if not aligned:
            value = damped(value, first_row, column)
        out_ref[:, columns] = value.astype(jnp.bfloat16)
    if aligned:
        side = min(tile, 256)
        for down in range(0, tile, side):
            columns = pl.ds(pl.multiple_of(step * tile + down, side), side)
            value = damped(scaled(left[down:down + side], columns), 0, 0)
            out_ref[pl.ds(down, side), columns] = value.astype(jnp.bfloat16)


def select_kernel(block_rows, slot_rows, ids_ref, window_ref, act_ref, out_ref):
    tokens, width = act_ref.shape
    per_expert = tokens // block_rows * slot_rows
    rows = WIN * per_expert

    def iota(shape, dim):
        return lax.broadcasted_iota(jnp.int32, shape, dim)

    ids, window = ids_ref[...], window_ref[...]
    matched = jnp.zeros((tokens, WIN), jnp.float32)
    for k in range(ids.shape[1]):
        matched += jnp.where(ids[:, k:k + 1] == window, 1.0, 0.0)
    matched = matched.astype(jnp.bfloat16)
    later, earlier = iota((tokens, tokens), 0), iota((tokens, tokens), 1)
    before = (earlier < later) & (earlier // block_rows == later // block_rows)
    place = jnp.dot(
        jnp.where(before, 1.0, 0.0).astype(jnp.bfloat16), matched, preferred_element_type=jnp.float32
    ).astype(jnp.bfloat16)
    spread = jnp.where(iota((rows, WIN), 0) // per_expert == iota((rows, WIN), 1), 1.0, 0.0).astype(jnp.bfloat16)
    dims = (((1,), (1,)), ((), ()))
    hit = lax.dot_general(spread, matched, dims, preferred_element_type=jnp.float32)
    position = lax.dot_general(spread, place, dims, preferred_element_type=jnp.float32)
    row, token = iota((rows, tokens), 0), iota((rows, tokens), 1)
    inside = row % per_expert
    taken = (
        (hit > 0.5)
        & (position.astype(jnp.int32) == inside % slot_rows)
        & (token // block_rows == inside // slot_rows)
    )
    chosen = jnp.where(taken, 1.0, 0.0)
    flags = jnp.sum(chosen, axis=1, keepdims=True)
    out_ref[:, width:] = jnp.broadcast_to(flags, (rows, FLAG)).astype(jnp.bfloat16)
    chosen = chosen.astype(jnp.bfloat16)
    for column in range(0, width, 512):
        columns = pl.ds(column, 512)
        out_ref[:, columns] = jnp.dot(
            chosen, act_ref[:, columns], preferred_element_type=jnp.float32
        ).astype(jnp.bfloat16)


def select_rows(expert_ids, window_experts, activations, block_rows, slot_rows):
    tokens, width = activations.shape
    per_expert = tokens // block_rows * slot_rows
    return pl.pallas_call(
        functools.partial(select_kernel, block_rows, slot_rows),
        out_shape=jax.ShapeDtypeStruct((WIN * per_expert, width + FLAG), jnp.bfloat16),
        in_specs=[pl.BlockSpec(memory_space=pltpu.VMEM)] * 3,
        out_specs=pl.BlockSpec(memory_space=pltpu.VMEM),
        compiler_params=pltpu.CompilerParams(vmem_limit_bytes=32 * 1024 * 1024),
        cost_estimate=pl.CostEstimate(
            flops=2 * WIN * per_expert * tokens * width, bytes_accessed=6 * tokens * width, transcendentals=0
        ),
        name="select_rows",
    )(expert_ids, window_experts.reshape(1, WIN), activations)


def factor(rows, width, flagged, block_index, group_size, name, part=(0, 1), held=None):
    depth = rows.shape[0]
    span = width // group_size
    tile = row_tile(span)
    aligned = group_size == 1
    left = rows if aligned else lax.dynamic_slice_in_dim(rows, block_index * span, span, 1)
    steps = span // tile
    first, last = part[0] * steps // part[1], (part[0] + 1) * steps // part[1]
    return pl.pallas_call(
        functools.partial(factor_kernel, width, tile, 512, aligned, first),
        out_shape=jax.ShapeDtypeStruct((span, width), jnp.bfloat16),
        grid=(last - first,),
        in_specs=[
            pl.BlockSpec(memory_space=pltpu.SMEM),
            pl.BlockSpec((depth, FLAG), lambda i: (0, flagged.shape[1] // FLAG - 1)),
            pl.BlockSpec((depth, tile), lambda i: (0, i + first)),
            pl.BlockSpec(rows.shape, lambda i: (0, 0)),
        ] + [pl.BlockSpec(memory_space=pl.ANY)] * (held is not None),
        input_output_aliases={} if held is None else {4: 0},
        out_specs=pl.BlockSpec((tile, width), lambda i: (i + first, 0)),
        scratch_shapes=[pltpu.SMEM((2,), jnp.float32)],
        compiler_params=pltpu.CompilerParams(vmem_limit_bytes=56 * 1024 * 1024),
        cost_estimate=pl.CostEstimate(
            flops=2 * depth * (last - first) * tile * width, bytes_accessed=2 * (last - first) * tile * width + 2 * depth * width, transcendentals=0
        ),
        name=name,
    )((block_index * span).astype(jnp.int32).reshape(1), flagged, left, rows, *([] if held is None else [held]))


def stack_kernel(*refs):
    depth = refs[0].shape[0]
    for k, piece in enumerate(refs[:-1]):
        refs[-1][k * depth:(k + 1) * depth, :] = piece[...]


def stack(pieces):
    depth, width = pieces[0].shape
    return pl.pallas_call(
        stack_kernel,
        out_shape=jax.ShapeDtypeStruct((len(pieces) * depth, width), pieces[0].dtype),
        in_specs=[pl.BlockSpec(memory_space=pltpu.VMEM)] * len(pieces),
        out_specs=pl.BlockSpec(memory_space=pltpu.VMEM),
        name="stack_rows",
    )(*pieces)


def shards(activations, gradients, expert_ids, window_experts):
    devices = lax.axis_size("dp")
    group_size = devices // WIN
    tok_rows = activations.shape[0]
    block_rows = tok_rows // group_size
    slot_rows = max(2, 2 * block_rows * TOPK // EXPERTS)
    width_in = activations.shape[1]
    width_grad = gradients.shape[2]
    pair_rows = block_rows * TOPK
    matched = (expert_ids[:, :, None] == window_experts[None, None, :]).astype(jnp.int32)
    matched = matched.reshape(group_size, pair_rows, WIN)
    upper = (jnp.arange(pair_rows)[:, None] <= jnp.arange(pair_rows)[None, :]).astype(jnp.bfloat16)
    running = jnp.einsum(
        "gaw,ab->gbw", matched.astype(jnp.bfloat16), upper, preferred_element_type=jnp.float32
    )
    ordinal = running - 1.0
    placed = (matched[..., None] == 1) & (
        ordinal[..., None] == jnp.arange(slot_rows, dtype=jnp.float32)[None, None, None, :]
    )
    chosen = placed.astype(jnp.bfloat16)
    in_sorted = select_rows(expert_ids, window_experts, activations, block_rows, slot_rows)
    grad_sorted = jnp.einsum(
        "gaws,gaf->wgsf",
        chosen,
        gradients.reshape(group_size, pair_rows, width_grad),
        preferred_element_type=jnp.float32,
    ).astype(jnp.bfloat16)
    copies_in = jnp.repeat(
        in_sorted.reshape(WIN, group_size * slot_rows, width_in + FLAG), group_size, axis=0
    )
    in_rows = lax.all_to_all(copies_in, "dp", split_axis=0, concat_axis=0, tiled=True)
    in_rows = in_rows.reshape(-1, width_in + FLAG)
    grad_blocks = grad_sorted.reshape(WIN, group_size * slot_rows, width_grad)
    if group_size == 1:
        me = lax.axis_index("dp")
        sends = [lax.dynamic_index_in_dim(grad_blocks, me ^ k, 0, keepdims=False) for k in range(devices)]
        in_rows, *sends = lax.optimization_barrier((in_rows, *sends))
        landed, held, parts = [sends[0]], None, 3
        sends = sends[1:]
        share = -(-len(sends) // parts)
        for part in range(parts):
            in_rows, *ready = lax.optimization_barrier((in_rows, *landed, *sends[part * share:]))
            landed, sends[part * share:] = list(ready[:len(landed)]), list(ready[len(landed):])
            for k in range(part * share + 1, min(devices, (part + 1) * share + 1)):
                landed.append(lax.ppermute(sends[k - 1], "dp", [(i, i ^ k) for i in range(devices)]))
            held = factor(in_rows, width_in, in_rows, me * 0, 1, "input_factor", (part, parts), held)
        grad_rows = stack(landed)
        return held, factor(grad_rows, width_grad, in_rows, me * 0, 1, "grad_factor")
    else:
        copies_grad = jnp.repeat(grad_blocks, group_size, axis=0)
        grad_rows = lax.all_to_all(copies_grad, "dp", split_axis=0, concat_axis=0, tiled=True)
        grad_rows = grad_rows.reshape(-1, width_grad)
    block_index = lax.axis_index("dp") % group_size
    return (
        factor(in_rows, width_in, in_rows, block_index, group_size, "input_factor"),
        factor(grad_rows, width_grad, in_rows, block_index, group_size, "grad_factor"),
    )


def solution(mesh):
    placed = (
        P(("groups", "dp"), None),
        P(("groups", "dp"), None, None),
        P(("groups", "dp"), None),
        P(),
    )
    return jax.shard_map(
        shards,
        mesh=mesh,
        in_specs=placed,
        out_specs=(P(("groups", "dp"), None), P(("groups", "dp"), None)),
        check_vma=False,
    )
```
